32 devices in a mesh: row: 4 (over x, core), col: 8 (over z, y).
Axes of the slice: x: 2, y: 2, z: 4, core: 2. Of those that a mesh axis runs over, the one named last changes fastest.
Arguments:
- features: bfloat16 [8192, 512], P(('col', 'row')), may hold values from -6 to 6
- weight: bfloat16 [512, 512], replicated, may hold values from -0.25 to 0.25
- entry_values: bfloat16 [4, 8, 32, 128, 128], P('row', 'col'), may hold values from 0.0009994507 to 0.019897461
- block_rows: int32 [4, 8, 32], P('row', 'col'), may hold values from 0 to 15
- block_cols: int32 [4, 8, 32], P('row', 'col'), may hold values from 0 to 7
- entry_counts: int32 [4, 8], P('row', 'col'), may hold values from 8 to 32, as said below
- cotangent: bfloat16 [8192, 512], P(('row', 'col')), may hold values from -1.5 to 1.5
Outputs:
- output: bfloat16 [8192, 512], P(('row', 'col'))
- grad_features: bfloat16 [8192, 512], P(('col', 'row'))
- grad_weight: float32 [512, 512], replicated
The draws below stay inside these ranges and needn't reach their ends.
Inputs may be any that keep to these rules, and one draw needn't show every extreme that they name: `entry_counts`: each grid cell has at least 8 live slots; at least one cell has all 32 live.
All inputs are finite; a program needn't handle non-finite values.
Results may differ from the reference program's by a relative error of at most 0.022.
Values may be sent and summed in bfloat16 or wider, within the bound.
A program may use at most 128 MiB of HBM per device.

```python
import math
import jax
import jax.numpy as jnp
from jax import lax

F = 512
BLOCK = 128
ROWS_DEV = 256
ENTRIES = 32
NODES = 8192
ROW_BLOCKS = 16
COL_BLOCKS = 8
N_ROW = 4
N_COL = 8


def draw_entry_counts(key, part):
    keys = jax.random.split(jax.random.fold_in(key, 7), 3)
    lowest = ENTRIES // 4
    first = jax.random.randint(keys[0], (N_ROW * N_COL,), lowest, ENTRIES + 1)
    second = jax.random.randint(keys[1], (N_ROW * N_COL,), lowest, ENTRIES + 1)
    chosen = jax.random.randint(keys[2], (), 0, N_ROW * N_COL)
    counts = jnp.where(jnp.arange(N_ROW * N_COL) == chosen, ENTRIES, jnp.minimum(first, second))
    return counts.reshape(N_ROW, N_COL).astype(jnp.int32)


def with_ends(values, rng, least, high):
    extent = values.shape
    spot = [jax.random.randint(jax.random.fold_in(rng, axis), (), 0, extent[axis]) for axis in range(len(extent))]
    values = values.at[tuple(spot)].set(least)
    longest = extent.index(max(extent))
    spot[longest] = (spot[longest] + 1) % extent[longest]
    return values.at[tuple(spot)].set(high)


def level_of(own_key, dims, cuts, smallest, high):
    factor_of = 1.0
    for dim, parts in cuts:
        draws = jax.random.uniform(jax.random.fold_in(jax.random.fold_in(own_key, 6), dim), (parts,), jnp.float32, smallest / len(cuts), high / len(cuts))
        factor_of = factor_of * jnp.repeat(jnp.exp(draws), dims[dim] // parts).reshape((-1,) + (1,) * (len(dims) - 1 - dim))
    return factor_of


def centred(key, shape, deviation, limit, shards=(), kind=jnp.bfloat16):
    array = jax.random.normal(key, shape, jnp.float32) * deviation
    if len(shards) > 0:
        array = level_of(key, shape, shards, -0.22, 0.18) * array
    return jnp.clip(array, min=-limit, max=limit).astype(kind)


def setup_inputs(seed: int = 0) -> dict:
    key_of = jax.random.split(jax.random.key(seed), 8)
    features = centred(key_of[0], (NODES, F), 1.0, 6.0, ((0, 32),))
    weight = centred(key_of[1], (F, F), F ** -0.5, 0.25)
    entry_values = jnp.clip(jnp.exp(math.log(0.019897461) - 2.9911416 * jax.random.uniform(key_of[2], (N_ROW, N_COL, ENTRIES, BLOCK, BLOCK), jnp.float32) ** level_of(key_of[2], (N_ROW, N_COL, ENTRIES, BLOCK, BLOCK), ((0, 4), (1, 8)), -0.2, 0.2)), 0.0009994507, 0.019897461).astype(jnp.bfloat16)
    block_rows = with_ends(jax.random.randint(key_of[3], (N_ROW, N_COL, ENTRIES), 0, ROW_BLOCKS), jax.random.fold_in(key_of[3], 1), 0, ROW_BLOCKS - 1).astype(jnp.int32)
    block_cols = with_ends(jax.random.randint(key_of[4], (N_ROW, N_COL, ENTRIES), 0, COL_BLOCKS), jax.random.fold_in(key_of[4], 1), 0, COL_BLOCKS - 1).astype(jnp.int32)
    entry_counts = draw_entry_counts(jax.random.fold_in(key_of[7], 71), 0)
    cotangent = centred(key_of[6], (NODES, F), 0.25, 1.5, ((0, 32),))
    return {"features": features, "weight": weight, "entry_values": entry_values, "block_rows": block_rows, "block_cols": block_cols, "entry_counts": entry_counts, "cotangent": cotangent}


def cell_sum(values, source_ids, target_ids, live_count, source, target_blocks, transpose):
    feature_count = source.shape[1]
    tiles = source.reshape(-1, BLOCK, feature_count)[source_ids].astype(jnp.float32)
    matrices = values.astype(jnp.float32)
    if transpose:
        products = jnp.einsum("kba,kbf->kaf", matrices, tiles)
    else:
        products = jnp.einsum("kab,kbf->kaf", matrices, tiles)
    alive_mask = (jnp.arange(ENTRIES) < live_count).astype(jnp.float32)
    selector = (target_ids[None, :] == jnp.arange(target_blocks)[:, None]).astype(jnp.float32) * alive_mask[None, :]
    running = jnp.einsum("rk,kaf->raf", selector, products, precision=lax.Precision.HIGHEST)
    return running.reshape(target_blocks * BLOCK, feature_count)


def rounded(value):
    return lax.optimization_barrier(value.astype(jnp.bfloat16)).astype(jnp.float32)


def reference(features, weight, entry_values, block_rows, block_cols, entry_counts, cotangent):
    projected = jnp.dot(features, weight, preferred_element_type=jnp.float32).astype(jnp.bfloat16)
    row_span = N_COL * ROWS_DEV
    col_span = N_ROW * ROWS_DEV

    def forward_row(i):
        def over_cols(j, running):
            start = (j * col_span).astype(jnp.int32)
            panel = lax.dynamic_slice_in_dim(projected, start, col_span, 0)
            term = cell_sum(entry_values[i, j], block_cols[i, j], block_rows[i, j], entry_counts[i, j], panel, ROW_BLOCKS, False)
            return running + rounded(term)
        return lax.fori_loop(0, N_COL, over_cols, jnp.zeros((row_span, F), jnp.float32))

    pre = lax.map(forward_row, jnp.arange(N_ROW, dtype=jnp.int32)).reshape(NODES, F)
    output = jax.nn.silu(pre).astype(jnp.bfloat16)
    sigmoid_value = jax.nn.sigmoid(pre)
    upstream = (cotangent.astype(jnp.float32) * sigmoid_value * (1.0 + pre * (1.0 - sigmoid_value))).astype(jnp.bfloat16)

    def backward_col(j):
        def over_rows(i, running):
            start = (i * row_span).astype(jnp.int32)
            panel = lax.dynamic_slice_in_dim(upstream, start, row_span, 0)
            term = cell_sum(entry_values[i, j], block_rows[i, j], block_cols[i, j], entry_counts[i, j], panel, COL_BLOCKS, True)
            return running + rounded(term)
        return lax.fori_loop(0, N_ROW, over_rows, jnp.zeros((col_span, F), jnp.float32))

    grad_projected = lax.map(backward_col, jnp.arange(N_COL, dtype=jnp.int32)).reshape(NODES, F).astype(jnp.bfloat16)
    grad_weight = jnp.dot(features.T, grad_projected, preferred_element_type=jnp.float32)
    grad_features = jnp.dot(grad_projected, weight.T, preferred_element_type=jnp.float32).astype(jnp.bfloat16)
    return (output, grad_features, grad_weight)
```

```python
import functools

import jax
import jax.numpy as jnp
from jax import lax
from jax.experimental import pallas as pl
from jax.experimental.pallas import tpu as pltpu
from jax.sharding import PartitionSpec as P

MESH = pl.DeviceIdType.MESH
BF = jnp.bfloat16
F32 = jnp.float32
VMEM_LIMIT = 60 * 1024 * 1024


def densify(values, rows, cols, count, dense):
    side = values.shape[1]
    per = dense.shape[1] // side

    def clear(j, carry):
        dense[j] = jnp.zeros(dense.shape[1:], dense.dtype)
        return carry

    lax.fori_loop(0, dense.shape[0], clear, 0)

    def add(k, carry):
        r, c = rows[k], cols[k]
        spot = (
            r // per,
            pl.ds(pl.multiple_of((r % per) * side, side), side),
            pl.ds(pl.multiple_of(c * side, side), side),
        )
        dense[spot] = (dense[spot].astype(F32) + values[k].astype(F32)).astype(dense.dtype)
        return carry

    lax.fori_loop(0, count[0], add, 0)


def dot(a, b, dims):
    return lax.dot_general(a, b, (dims, ((), ())), preferred_element_type=F32)


NN = ((1,), (0,))
TN = ((0,), (0,))
NT = ((1,), (1,))


def layer(n_row, n_col, feat, weight, dense, cot, out, gfeat, gweight, s):
    ri_n = 2
    ro_n = n_row // ri_n
    co_n = 4
    ci_n = n_col // co_n
    rows, width = feat.shape
    r, c = lax.axis_index("row"), lax.axis_index("col")
    ro, ri = r // ri_n, r % ri_n
    co, ci = c // ci_n, c % ci_n
    span = n_row * rows

    def send(src, dst, ss, rs, row, col):
        return pltpu.make_async_remote_copy(
            src_ref=src, dst_ref=dst, send_sem=ss, recv_sem=rs, device_id=(row, col), device_id_type=MESH
        )

    def arrived(dst, rs, ss):
        send(dst, dst, ss, rs, r, lax.rem(c + 1, n_col)).wait_recv()

    barrier = pltpu.get_barrier_semaphore()
    for d in range(1, n_row):
        pl.semaphore_signal(barrier, inc=1, device_id=(lax.rem(r + d, n_row), c), device_id_type=MESH)
    for d in range(1, n_col):
        pl.semaphore_signal(barrier, inc=1, device_id=(r, lax.rem(c + d, n_col)), device_id_type=MESH)
    pl.semaphore_wait(barrier, n_row + n_col - 2)

    mate = ro * ri_n + (1 - ri)
    pending = []
    for d in range(1, ro_n):
        peer = lax.rem(ro + d, ro_n) * ri_n + ri
        cp = send(feat, s["panel"].at[r], s["pss"].at[d - 1], s["prs"].at[r], peer, c)
        cp.start()
        pending.append(cp)
    cp = send(feat, s["panel"].at[r], s["pss"].at[ro_n - 1], s["prs"].at[r], mate, c)
    cp.start()
    pending.append(cp)
    s["panel"][r] = feat[...]

    def project(slot):
        s["proj"][slot] = dot(s["panel"][slot], weight[...], NN).astype(BF)

    project(r)
    for d in range(1, ro_n):
        slot = lax.rem(ro - d + ro_n, ro_n) * ri_n + ri
        arrived(s["panel"].at[slot], s["prs"].at[slot], s["pss"].at[0])
        cp = send(s["panel"].at[slot], s["panel"].at[slot], s["pss"].at[ro_n - 1 + d], s["prs"].at[slot], mate, c)
        cp.start()
        pending.append(cp)
        project(slot)
    for d in range(ro_n):
        slot = lax.rem(ro - d + ro_n, ro_n) * ri_n + (1 - ri)
        arrived(s["panel"].at[slot], s["prs"].at[slot], s["pss"].at[0])
        project(slot)

    def far(k):
        table = ((3, 2, 1, 0), (3, 0, 2, 1), (0, 3, 1, 2), (0, 1, 2, 3))

        def entry(pos):
            picked = jnp.int32(table[pos][co_n - 1])
            for q in range(co_n - 1):
                picked = jnp.where(k == q, table[pos][q], picked)
            return picked

        picked = entry(co_n - 1)
        for pos in range(co_n - 1):
            picked = jnp.where(co == pos, entry(pos), picked)
        return picked

    def fetch(j, slot):
        return pltpu.make_async_copy(dense.at[j], s["tile"].at[slot], s["ts"].at[slot])

    fetch(far(0) * ci_n + lax.rem(ci + 1, ci_n), 0).start()

    def forward(k, carry):
        t = far(k)
        for d in list(range(1, ci_n)) + [0]:
            step = k * ci_n + (d - 1 if d else ci_n - 1)
            slot = step % 2
            target = lax.rem(ci + d, ci_n)
            j = t * ci_n + target
            ahead = step + 1
            if d:
                after = t * ci_n + lax.rem(ci + (d + 1) % ci_n, ci_n)
                fetch(after, ahead % 2).start()
            else:
                @pl.when(k < co_n - 1)
                def _():
                    fetch(far(k + 1) * ci_n + lax.rem(ci + 1, ci_n), ahead % 2).start()
            fetch(j, slot).wait()
            part = dot(s["tile"][slot], s["proj"][...].reshape(span, width), NN)
            if d:
                s["ysend"][t, d - 1] = part.astype(BF)
                send(
                    s["ysend"].at[t, d - 1], s["yrecv"].at[t, d - 1], s["yss"].at[t, d - 1],
                    s["yrs"].at[t, d - 1], r, co * ci_n + target,
                ).start()
            else:
                s["mine"][t] = part
            s["spread"][j] = dot(s["tile"][slot], s["panel"][...].reshape(span, width), NN).astype(BF)
        return carry

    lax.fori_loop(0, co_n, forward, 0)

    def along(k, carry):
        t = far(k)
        for d in range(1, ci_n):
            arrived(s["yrecv"].at[t, d - 1], s["yrs"].at[t, d - 1], s["yss"].at[t, d - 1])
            s["mine"][t] = s["mine"][t] + s["yrecv"][t, d - 1].astype(F32)

        @pl.when(jnp.logical_and(t >= co, co > 0))
        def _():
            arrived(s["rrecv"].at[t], s["rrs"].at[t], s["lss"].at[t])
            s["mine"][t] = s["mine"][t] + s["rrecv"][t].astype(F32)

        @pl.when(jnp.logical_and(t <= co, co < co_n - 1))
        def _():
            arrived(s["lrecv"].at[t], s["lrs"].at[t], s["lss"].at[t])
            s["mine"][t] = s["mine"][t] + s["lrecv"][t].astype(F32)

        @pl.when(t != co)
        def _():
            s["lsend"][t] = s["mine"][t].astype(BF)

        @pl.when(t > co)
        def _():
            send(s["lsend"].at[t], s["rrecv"].at[t], s["lss"].at[t], s["rrs"].at[t], r, c + ci_n).start()

        @pl.when(t < co)
        def _():
            send(s["lsend"].at[t], s["lrecv"].at[t], s["lss"].at[t], s["lrs"].at[t], r, c - ci_n).start()

        return carry

    lax.fori_loop(0, co_n, along, 0)

    pre = s["mine"][co]
    sig = jax.nn.sigmoid(pre)
    s["up"][c] = (cot[...].astype(F32) * sig * (1.0 + pre * (1.0 - sig))).astype(BF)

    s["back"][...] = jnp.zeros(s["back"].shape, F32)
    s["gw"][...] = jnp.zeros(s["gw"].shape, F32)

    def upcopy(slot, kind, row, col):
        return send(s["up"].at[slot], s["up"].at[slot], s["uss"].at[slot, kind], s["urs"].at[slot], row, col)

    def use(j):
        fetch(j, 0).wait()
        u = s["up"][j]

        def piece(q, carry):
            cols = pl.ds(pl.multiple_of(q * rows, rows), rows)
            s["back"][q] = s["back"][q] + dot(s["tile"][0, :, cols], u, TN)
            return carry

        lax.fori_loop(0, n_row, piece, 0)
        s["gw"][...] = s["gw"][...] + dot(s["spread"][j], u, TN)

    def collect(j):
        fetch(j, 0).start()
        arrived(s["up"].at[j], s["urs"].at[j], s["uss"].at[j, 0])
        use(j)

    def backward(k, carry):
        t = far(co_n - 1 - k)
        j = t * ci_n + ci
        fetch(j, 0).start()

        @pl.when(k > 0)
        def _():
            arrived(s["up"].at[j], s["urs"].at[j], s["uss"].at[j, 0])

        @pl.when(jnp.logical_and(t <= co, co < co_n - 1))
        def _():
            upcopy(j, 0, r, c + ci_n).start()

        @pl.when(jnp.logical_and(t >= co, co > 0))
        def _():
            upcopy(j, 1, r, c - ci_n).start()

        for d in range(1, ci_n):
            upcopy(j, 1 + d, r, co * ci_n + lax.rem(ci + d, ci_n)).start()

        @pl.when(k == 0)
        def _():
            value = s["mine"][co]
            out[...] = (value * jax.nn.sigmoid(value)).astype(BF)

        use(j)

        @pl.when(k > 0)
        def _():
            before = far(co_n - k)
            for d in range(1, ci_n):
                collect(before * ci_n + lax.rem(ci + d, ci_n))

        return carry

    lax.fori_loop(0, co_n, backward, 0)
    for d in range(1, ci_n):
        collect(far(0) * ci_n + lax.rem(ci + d, ci_n))

    height = width // n_row
    s["gsend"][...] = s["gw"][...].astype(BF).reshape(n_row, height, width)
    for d in range(1, n_row):
        peer = lax.rem(r + d, n_row)
        cp = send(s["gsend"].at[peer], s["grecv"].at[d - 1], s["gss"].at[d - 1], s["grs"].at[d - 1], peer, c)
        cp.start()
        pending.append(cp)

    for q in range(ro_n):
        d = lax.rem(ro + 1 + q, ro_n)
        s["bsend"][d] = s["back"][d * ri_n + (1 - ri)].astype(BF)
        cp = send(s["bsend"].at[d], s["brecv"].at[d], s["bss"].at[d], s["brs"].at[d], mate, c)
        cp.start()
        pending.append(cp)
    for q in range(1, ro_n):
        d = lax.rem(ro + q, ro_n)
        arrived(s["brecv"].at[d], s["brs"].at[d], s["bss"].at[d])
        s["xsend"][q - 1] = (s["back"][d * ri_n + ri] + s["brecv"][d].astype(F32)).astype(BF)
        cp = send(
            s["xsend"].at[q - 1], s["xrecv"].at[q - 1], s["xss"].at[q - 1], s["xrs"].at[q - 1], d * ri_n + ri, c
        )
        cp.start()
        pending.append(cp)
    arrived(s["brecv"].at[ro], s["brs"].at[ro], s["bss"].at[ro])

    groups = s["part"].shape[0]
    thin = s["part"].shape[1]
    total = s["gsend"][r].astype(F32)
    for d in range(1, n_row):
        arrived(s["grecv"].at[d - 1], s["grs"].at[d - 1], s["gss"].at[d - 1])
        total = total + s["grecv"][d - 1].astype(F32)
    s["part"][...] = total.astype(BF).reshape(groups, thin, width)
    own = c % groups
    for d in range(1, n_col):
        peer = lax.rem(c + d, n_col)
        cp = send(s["part"].at[peer % groups], s["crecv"].at[c], s["css"].at[d - 1], s["crs"].at[c], r, peer)
        cp.start()
        pending.append(cp)
    s["crecv"][c] = s["part"][own]

    grad = s["back"][r] + s["brecv"][ro].astype(F32)
    for q in range(1, ro_n):
        arrived(s["xrecv"].at[q - 1], s["xrs"].at[q - 1], s["xss"].at[q - 1])
        grad = grad + s["xrecv"][q - 1].astype(F32)
    gfeat[...] = dot(grad.astype(BF), weight[...], NT).astype(BF)

    for d in range(1, n_col):
        slot = lax.rem(c + d, n_col)
        arrived(s["crecv"].at[slot], s["crs"].at[slot], s["css"].at[0])
    total = s["crecv"][0].astype(F32)
    for q in range(1, n_col):
        total = total + s["crecv"][q].astype(F32)
    place = pl.ds(pl.multiple_of(own * thin, thin), thin)
    s["full"][r, place, :] = total.astype(BF)
    for d in range(1, groups):
        peer = (c // groups) * groups + lax.rem(own + d, groups)
        cp = send(
            s["full"].at[r, place, :], s["full"].at[r, place, :], s["dss"].at[d], s["drs"].at[own], r, peer
        )
        cp.start()
        pending.append(cp)
    for d in range(1, groups):
        slot = lax.rem(own + d, groups)
        arrived(
            s["full"].at[r, pl.ds(pl.multiple_of(slot * thin, thin), thin), :], s["drs"].at[slot], s["dss"].at[0]
        )
    for d in range(1, n_row):
        cp = send(s["full"].at[r], s["full"].at[r], s["ess"].at[d], s["ers"].at[r], lax.rem(r + d, n_row), c)
        cp.start()
        pending.append(cp)
    for d in range(1, n_row):
        slot = lax.rem(r + d, n_row)
        arrived(s["full"].at[slot], s["ers"].at[slot], s["ess"].at[0])
    gweight[...] = s["full"][...].reshape(width, width).astype(F32)

    def left(k, carry):
        for d in range(1, ci_n):
            send(
                s["ysend"].at[k, d - 1], s["yrecv"].at[k, d - 1], s["yss"].at[k, d - 1], s["yrs"].at[k, d - 1],
                r, lax.rem(c + 1, n_col),
            ).wait_send()
            upcopy(k * ci_n + ci, 1 + d, r, lax.rem(c + 1, n_col)).wait_send()

        @pl.when(k != co)
        def _():
            send(s["lsend"].at[k], s["rrecv"].at[k], s["lss"].at[k], s["rrs"].at[k], r, lax.rem(c + 1, n_col)).wait_send()

        @pl.when(jnp.logical_and(k <= co, co < co_n - 1))
        def _():
            upcopy(k * ci_n + ci, 0, r, lax.rem(c + 1, n_col)).wait_send()

        @pl.when(jnp.logical_and(k >= co, co > 0))
        def _():
            upcopy(k * ci_n + ci, 1, r, lax.rem(c + 1, n_col)).wait_send()

        return carry

    lax.fori_loop(0, co_n, left, 0)
    for cp in pending:
        cp.wait_send()


def solution(mesh):
    n_row, n_col = mesh.shape["row"], mesh.shape["col"]

    def shards(features, weight, entry_values, block_rows, block_cols, entry_counts, cotangent):
        rows, width = features.shape
        span = n_row * rows
        co_n, ci_n, ro_n = 4, n_col // 4, n_row // 2
        smem = pl.BlockSpec(memory_space=pltpu.SMEM)
        vmem = pl.BlockSpec(memory_space=pltpu.VMEM)
        dense = pl.pallas_call(
            densify,
            out_shape=jax.ShapeDtypeStruct((n_col, rows, span), BF),
            in_specs=[vmem, smem, smem, smem],
            out_specs=vmem,
            compiler_params=pltpu.CompilerParams(vmem_limit_bytes=VMEM_LIMIT),
        )(entry_values[0, 0], block_rows[0, 0], block_cols[0, 0], entry_counts[0])

        height = width // n_row
        groups = min(n_col, height // 16)
        thin = height // groups
        block = (rows, width)
        sem = pltpu.SemaphoreType.DMA
        scratch = {
            "panel": pltpu.VMEM((n_row,) + block, BF),
            "proj": pltpu.VMEM((n_row,) + block, BF),
            "pss": sem((2 * ro_n,)),
            "prs": sem((n_row,)),
            "tile": pltpu.VMEM((2, rows, span), BF),
            "ts": sem((2,)),
            "ysend": pltpu.VMEM((co_n, ci_n - 1) + block, BF),
            "yrecv": pltpu.VMEM((co_n, ci_n - 1) + block, BF),
            "yss": sem((co_n, ci_n - 1)),
            "yrs": sem((co_n, ci_n - 1)),
            "mine": pltpu.VMEM((co_n,) + block, F32),
            "spread": pltpu.VMEM((n_col,) + block, BF),
            "lsend": pltpu.VMEM((co_n,) + block, BF),
            "rrecv": pltpu.VMEM((co_n,) + block, BF),
            "lrecv": pltpu.VMEM((co_n,) + block, BF),
            "lss": sem((co_n,)),
            "rrs": sem((co_n,)),
            "lrs": sem((co_n,)),
            "up": pltpu.VMEM((n_col,) + block, BF),
            "uss": sem((n_col, ci_n + 1)),
            "urs": sem((n_col,)),
            "back": pltpu.VMEM((n_row,) + block, F32),
            "gw": pltpu.VMEM((width, width), F32),
            "gsend": pltpu.VMEM((n_row, height, width), BF),
            "grecv": pltpu.VMEM((n_row - 1, height, width), BF),
            "gss": sem((n_row - 1,)),
            "grs": sem((n_row - 1,)),
            "bsend": pltpu.VMEM((ro_n,) + block, BF),
            "brecv": pltpu.VMEM((ro_n,) + block, BF),
            "bss": sem((ro_n,)),
            "brs": sem((ro_n,)),
            "xsend": pltpu.VMEM((ro_n - 1,) + block, BF),
            "xrecv": pltpu.VMEM((ro_n - 1,) + block, BF),
            "xss": sem((ro_n - 1,)),
            "xrs": sem((ro_n - 1,)),
            "part": pltpu.VMEM((groups, thin, width), BF),
            "crecv": pltpu.VMEM((n_col, thin, width), BF),
            "css": sem((n_col - 1,)),
            "crs": sem((n_col,)),
            "full": pltpu.VMEM((n_row, height, width), BF),
            "dss": sem((groups,)),
            "drs": sem((groups,)),
            "ess": sem((n_row,)),
            "ers": sem((n_row,)),
        }
        names = list(scratch)

        def kernel(feat, w, a, cot, out, gfeat, gweight, *refs):
            layer(n_row, n_col, feat, w, a, cot, out, gfeat, gweight, dict(zip(names, refs)))

        return tuple(
            pl.pallas_call(
                kernel,
                out_shape=(
                    jax.ShapeDtypeStruct(block, BF),
                    jax.ShapeDtypeStruct(block, BF),
                    jax.ShapeDtypeStruct((width, width), F32),
                ),
                in_specs=[vmem, vmem, pl.BlockSpec(memory_space=pl.ANY), vmem],
                out_specs=(vmem, vmem, vmem),
                scratch_shapes=[scratch[name] for name in names],
                compiler_params=pltpu.CompilerParams(
                    collective_id=0, has_side_effects=True, vmem_limit_bytes=VMEM_LIMIT
                ),
            )(features, weight, dense, cotangent)
        )

    return jax.shard_map(
        shards,
        mesh=mesh,
        in_specs=(
            P(("col", "row"), None),
            P(),
            P("row", "col", None, None, None),
            P("row", "col", None),
            P("row", "col", None),
            P("row", "col"),
            P(("row", "col"), None),
        ),
        out_specs=(P(("row", "col"), None), P(("col", "row"), None), P()),
        check_vma=False,
    )
```

```python
import functools

import jax
import jax.numpy as jnp
from jax import lax
from jax.experimental import pallas as pl
from jax.experimental.pallas import tpu as pltpu
from jax.sharding import PartitionSpec as P

MESH = pl.DeviceIdType.MESH
BF = jnp.bfloat16
F32 = jnp.float32
VMEM_LIMIT = 60 * 1024 * 1024
PIECES = 2


def densify(values, rows, cols, count, dense):
    side = values.shape[1]
    per = dense.shape[1] // side

    def clear(j, carry):
        dense[j] = jnp.zeros(dense.shape[1:], dense.dtype)
        return carry

    lax.fori_loop(0, dense.shape[0], clear, 0)

    def add(k, carry):
        r, c = rows[k], cols[k]
        spot = (
            r // per,
            pl.ds(pl.multiple_of((r % per) * side, side), side),
            pl.ds(pl.multiple_of(c * side, side), side),
        )
        dense[spot] = (dense[spot].astype(F32) + values[k].astype(F32)).astype(dense.dtype)
        return carry

    lax.fori_loop(0, count[0], add, 0)


def dot(a, b, dims):
    return lax.dot_general(a, b, (dims, ((), ())), preferred_element_type=F32)


NN = ((1,), (0,))
TN = ((0,), (0,))
NT = ((1,), (1,))


def finish(out_in, gfeat_in, gweight_in, out, gfeat, gweight):
    out[...] = out_in[...]
    gfeat[...] = gfeat_in[...]
    gweight[...] = gweight_in[...].astype(F32)


def layer(n_row, n_col, feat, weight_in, dense, cot_in, out, gfeat, gweight, s):
    ri_n = 2
    ro_n = n_row // ri_n
    co_n = 4
    ci_n = n_col // co_n
    rows, width = feat.shape
    r, c = lax.axis_index("row"), lax.axis_index("col")
    ro, ri = r // ri_n, r % ri_n
    co, ci = c // ci_n, c % ci_n
    span = n_row * rows
    thick = rows // PIECES
    cuts = [pl.ds(h * thick, thick) for h in range(PIECES)]
    weight, cot = s["weight"], s["cot"]

    def send(src, dst, ss, rs, row, col):
        return pltpu.make_async_remote_copy(
            src_ref=src, dst_ref=dst, send_sem=ss, recv_sem=rs, device_id=(row, col), device_id_type=MESH
        )

    def arrived(dst, rs, ss):
        send(dst, dst, ss, rs, r, lax.rem(c + 1, n_col)).wait_recv()

    barrier = pltpu.get_barrier_semaphore()
    for d in range(1, n_row):
        pl.semaphore_signal(barrier, inc=1, device_id=(lax.rem(r + d, n_row), c), device_id_type=MESH)
    for d in range(1, n_col):
        pl.semaphore_signal(barrier, inc=1, device_id=(r, lax.rem(c + d, n_col)), device_id_type=MESH)
    loads = [
        pltpu.make_async_copy(feat, s["panel"].at[r], s["ls"].at[0]),
        pltpu.make_async_copy(weight_in, weight, s["ls"].at[1]),
        pltpu.make_async_copy(cot_in, cot, s["ls"].at[2]),
    ]
    for cp in loads:
        cp.start()
    pl.semaphore_wait(barrier, n_row + n_col - 2)

    mate = ro * ri_n + (1 - ri)
    pending = []
    for d in range(1, ro_n):
        peer = lax.rem(ro + d, ro_n) * ri_n + ri
        cp = send(feat, s["panel"].at[r], s["pss"].at[d - 1], s["prs"].at[r], peer, c)
        cp.start()
        pending.append(cp)
    cp = send(feat, s["panel"].at[r], s["pss"].at[ro_n - 1], s["prs"].at[r], mate, c)
    cp.start()
    pending.append(cp)

    def far(k):
        table = ((3, 2, 1, 0), (3, 0, 2, 1), (0, 3, 1, 2), (0, 1, 2, 3))

        def entry(pos):
            picked = jnp.int32(table[pos][co_n - 1])
            for q in range(co_n - 1):
                picked = jnp.where(k == q, table[pos][q], picked)
            return picked

        picked = entry(co_n - 1)
        for pos in range(co_n - 1):
            picked = jnp.where(co == pos, entry(pos), picked)
        return picked

    def fetch(j, slot):
        return pltpu.make_async_copy(dense.at[j], s["tile"].at[slot], s["ts"].at[slot])

    fetch(far(0) * ci_n + lax.rem(ci + 1, ci_n), 0).start()
    for cp in loads:
        cp.wait()

    def project(slot):
        s["proj"][slot] = dot(s["panel"][slot], weight[...], NN).astype(BF)

    project(r)
    for d in range(1, ro_n):
        slot = lax.rem(ro - d + ro_n, ro_n) * ri_n + ri
        arrived(s["panel"].at[slot], s["prs"].at[slot], s["pss"].at[0])
        cp = send(s["panel"].at[slot], s["panel"].at[slot], s["pss"].at[ro_n - 1 + d], s["prs"].at[slot], mate, c)
        cp.start()
        pending.append(cp)
        project(slot)
    for d in range(ro_n):
        slot = lax.rem(ro - d + ro_n, ro_n) * ri_n + (1 - ri)
        arrived(s["panel"].at[slot], s["prs"].at[slot], s["pss"].at[0])
        project(slot)

    def ycopy(t, d, h, col):
        return send(
            s["ysend"].at[t, d, cuts[h]], s["yrecv"].at[t, d, cuts[h]], s["yss"].at[t, d, h], s["yrs"].at[t, d, h],
            r, col,
        )

    def lcopy(t, h, name, col):
        return send(
            s["lsend"].at[t, cuts[h]], s[name + "recv"].at[t, cuts[h]], s["lss"].at[t, h], s[name + "rs"].at[t, h],
            r, col,
        )

    other = lax.rem(c + 1, n_col)

    def forward(k, carry):
        t = far(k)
        for d in list(range(1, ci_n)) + [0]:
            step = k * ci_n + (d - 1 if d else ci_n - 1)
            slot = step % 2
            target = lax.rem(ci + d, ci_n)
            j = t * ci_n + target
            ahead = step + 1
            if d:
                after = t * ci_n + lax.rem(ci + (d + 1) % ci_n, ci_n)
                fetch(after, ahead % 2).start()
            else:
                @pl.when(k < co_n - 1)
                def _():
                    fetch(far(k + 1) * ci_n + lax.rem(ci + 1, ci_n), ahead % 2).start()
            fetch(j, slot).wait()
            part = dot(s["tile"][slot], s["proj"][...].reshape(span, width), NN)
            if d:
                s["ysend"][t, d - 1] = part.astype(BF)
                for h in range(PIECES):
                    ycopy(t, d - 1, h, co * ci_n + target).start()
            else:
                s["mine"][t] = part
            s["spread"][j] = dot(s["tile"][slot], s["panel"][...].reshape(span, width), NN).astype(BF)
        return carry

    lax.fori_loop(0, co_n, forward, 0)

    def along(k, carry):
        t = far(k)
        for h in range(PIECES):
            cut = cuts[h]
            for d in range(1, ci_n):
                ycopy(t, d - 1, h, other).wait_recv()
                s["mine"][t, cut] = s["mine"][t, cut] + s["yrecv"][t, d - 1, cut].astype(F32)

            @pl.when(jnp.logical_and(t >= co, co > 0))
            def _():
                lcopy(t, h, "r", other).wait_recv()
                s["mine"][t, cut] = s["mine"][t, cut] + s["rrecv"][t, cut].astype(F32)

            @pl.when(jnp.logical_and(t <= co, co < co_n - 1))
            def _():
                lcopy(t, h, "l", other).wait_recv()
                s["mine"][t, cut] = s["mine"][t, cut] + s["lrecv"][t, cut].astype(F32)

            @pl.when(t != co)
            def _():
                s["lsend"][t, cut] = s["mine"][t, cut].astype(BF)

            @pl.when(t > co)
            def _():
                lcopy(t, h, "r", c + ci_n).start()

            @pl.when(t < co)
            def _():
                lcopy(t, h, "l", c - ci_n).start()

        return carry

    lax.fori_loop(0, co_n, along, 0)

    pre = s["mine"][co]
    sig = jax.nn.sigmoid(pre)
    s["up"][c] = (cot[...].astype(F32) * sig * (1.0 + pre * (1.0 - sig))).astype(BF)

    s["back"][...] = jnp.zeros(s["back"].shape, F32)
    s["gw"][...] = jnp.zeros(s["gw"].shape, F32)

    def upcopy(slot, h, kind, row, col):
        return send(
            s["up"].at[slot, cuts[h]], s["up"].at[slot, cuts[h]], s["uss"].at[slot, h, kind], s["urs"].at[slot, h],
            row, col,
        )

    def use_back(j, slot):
        fetch(j, slot).wait()
        u = s["up"][j]

        def piece(q, carry):
            cols = pl.ds(pl.multiple_of(q * rows, rows), rows)
            s["back"][q] = s["back"][q] + dot(s["tile"][slot, :, cols], u, TN)
            return carry

        lax.fori_loop(0, n_row, piece, 0)

    def use_gw(j):
        s["gw"][...] = s["gw"][...] + dot(s["spread"][j], s["up"][j], TN)

    def wait_up(j):
        for h in range(PIECES):
            upcopy(j, h, 0, r, other).wait_recv()

    def pass_on(k, h):
        t = far(co_n - 1 - k)
        j = t * ci_n + ci

        @pl.when(k > 0)
        def _():
            upcopy(j, h, 0, r, other).wait_recv()

        @pl.when(jnp.logical_and(t <= co, co < co_n - 1))
        def _():
            upcopy(j, h, 0, r, c + ci_n).start()

        @pl.when(jnp.logical_and(t >= co, co > 0))
        def _():
            upcopy(j, h, 1, r, c - ci_n).start()

        for d in range(1, ci_n):
            upcopy(j, h, 1 + d, r, co * ci_n + lax.rem(ci + d, ci_n)).start()

    def own_chunk(k):
        return far(co_n - 1 - k) * ci_n + ci

    def side_chunk(k, d):
        return far(co_n - 1 - k) * ci_n + lax.rem(ci + d, ci_n)

    def use_own(k):
        j = own_chunk(k)
        use_back(j, 0)
        use_gw(j)

    def use_sides(k):
        for d in range(1, ci_n):
            j = side_chunk(k, d)
            fetch(j, 1).start()
            wait_up(j)
            use_back(j, 1)
            use_gw(j)

    def backward(k, carry):
        @pl.when(k > 0)
        def _():
            fetch(own_chunk(k - 1), 0).start()

        for h in range(PIECES - 1):
            pass_on(k, h)

        @pl.when(k > 0)
        def _():
            use_own(k - 1)

        pass_on(k, PIECES - 1)

        @pl.when(k == 0)
        def _():
            value = s["mine"][co]
            out[...] = (value * jax.nn.sigmoid(value)).astype(BF)

        @pl.when(k > 1)
        def _():
            use_sides(k - 2)

        return carry

    lax.fori_loop(0, co_n, backward, 0)
    fetch(own_chunk(co_n - 1), 0).start()
    use_own(co_n - 1)
    use_sides(co_n - 2)
    for d in range(1, ci_n):
        last = side_chunk(co_n - 1, d)
        fetch(last, 1).start()
        wait_up(last)
        if d < ci_n - 1:
            use_back(last, 1)
        use_gw(last)

    height = width // n_row
    s["gsend"][...] = s["gw"][...].astype(BF).reshape(n_row, height, width)
    for d in range(1, n_row):
        peer = lax.rem(r + d, n_row)
        cp = send(s["gsend"].at[peer], s["grecv"].at[d - 1], s["gss"].at[d - 1], s["grs"].at[d - 1], peer, c)
        cp.start()
        pending.append(cp)

    use_back(last, 1)

    for q in range(ro_n):
        d = lax.rem(ro + 1 + q, ro_n)
        s["bsend"][d] = s["back"][d * ri_n + (1 - ri)].astype(BF)
        cp = send(s["bsend"].at[d], s["brecv"].at[d], s["bss"].at[d], s["brs"].at[d], mate, c)
        cp.start()
        pending.append(cp)
    for q in range(1, ro_n):
        d = lax.rem(ro + q, ro_n)
        arrived(s["brecv"].at[d], s["brs"].at[d], s["bss"].at[d])
        s["xsend"][q - 1] = (s["back"][d * ri_n + ri] + s["brecv"][d].astype(F32)).astype(BF)
        cp = send(
            s["xsend"].at[q - 1], s["xrecv"].at[q - 1], s["xss"].at[q - 1], s["xrs"].at[q - 1], d * ri_n + ri, c
        )
        cp.start()
        pending.append(cp)
    arrived(s["brecv"].at[ro], s["brs"].at[ro], s["bss"].at[ro])

    groups = s["part"].shape[0]
    thin = s["part"].shape[1]
    total = s["gsend"][r].astype(F32)
    for d in range(1, n_row):
        arrived(s["grecv"].at[d - 1], s["grs"].at[d - 1], s["gss"].at[d - 1])
        total = total + s["grecv"][d - 1].astype(F32)
    s["part"][...] = total.astype(BF).reshape(groups, thin, width)
    own = c % groups
    for d in range(1, n_col):
        peer = lax.rem(c + d, n_col)
        cp = send(s["part"].at[peer % groups], s["crecv"].at[c], s["css"].at[d - 1], s["crs"].at[c], r, peer)
        cp.start()
        pending.append(cp)
    s["crecv"][c] = s["part"][own]

    grad = s["back"][r] + s["brecv"][ro].astype(F32)
    for q in range(1, ro_n):
        arrived(s["xrecv"].at[q - 1], s["xrs"].at[q - 1], s["xss"].at[q - 1])
        grad = grad + s["xrecv"][q - 1].astype(F32)
    gfeat[...] = dot(grad.astype(BF), weight[...], NT).astype(BF)

    for d in range(1, n_col):
        slot = lax.rem(c + d, n_col)
        arrived(s["crecv"].at[slot], s["crs"].at[slot], s["css"].at[0])
    total = s["crecv"][0].astype(F32)
    for q in range(1, n_col):
        total = total + s["crecv"][q].astype(F32)
    place = pl.ds(pl.multiple_of(own * thin, thin), thin)
    s["full"][r, place, :] = total.astype(BF)
    def strip(row, piece):
        return s["full"].at[row, pl.ds(pl.multiple_of(piece * thin, thin), thin), :]

    def spread_rows(piece):
        for d in range(1, n_row):
            peer = lax.rem(r + d, n_row)
            ref = strip(r, piece)
            cp = send(ref, ref, s["ess"].at[d, piece], s["ers"].at[r, piece], peer, c)
            cp.start()
            pending.append(cp)

    for d in range(1, groups):
        peer = (c // groups) * groups + lax.rem(own + d, groups)
        cp = send(strip(r, own), strip(r, own), s["dss"].at[d], s["drs"].at[own], r, peer)
        cp.start()
        pending.append(cp)
    spread_rows(own)
    for d in range(1, groups):
        slot = lax.rem(own + groups - d, groups)
        arrived(strip(r, slot), s["drs"].at[slot], s["dss"].at[0])
        spread_rows(slot)
    for d in range(1, n_row):
        row = lax.rem(r + d, n_row)
        for piece in range(groups):
            arrived(strip(row, piece), s["ers"].at[row, piece], s["ess"].at[0, 0])
    gweight[...] = s["full"][...].reshape(width, width)

    def left(k, carry):
        j = k * ci_n + ci
        for h in range(PIECES):
            for d in range(1, ci_n):
                ycopy(k, d - 1, h, other).wait_send()
                upcopy(j, h, 1 + d, r, other).wait_send()

            @pl.when(k != co)
            def _():
                lcopy(k, h, "r", other).wait_send()

            @pl.when(jnp.logical_and(k <= co, co < co_n - 1))
            def _():
                upcopy(j, h, 0, r, other).wait_send()

            @pl.when(jnp.logical_and(k >= co, co > 0))
            def _():
                upcopy(j, h, 1, r, other).wait_send()

        return carry

    lax.fori_loop(0, co_n, left, 0)
    for cp in pending:
        cp.wait_send()


def solution(mesh):
    n_row, n_col = mesh.shape["row"], mesh.shape["col"]

    def shards(features, weight, entry_values, block_rows, block_cols, entry_counts, cotangent):
        rows, width = features.shape
        span = n_row * rows
        co_n, ci_n, ro_n = 4, n_col // 4, n_row // 2
        smem = pl.BlockSpec(memory_space=pltpu.SMEM)
        vmem = pl.BlockSpec(memory_space=pltpu.VMEM)
        dense = pl.pallas_call(
            densify,
            out_shape=jax.ShapeDtypeStruct((n_col, rows, span), BF),
            in_specs=[vmem, smem, smem, smem],
            out_specs=vmem,
            compiler_params=pltpu.CompilerParams(vmem_limit_bytes=VMEM_LIMIT),
        )(entry_values[0, 0], block_rows[0, 0], block_cols[0, 0], entry_counts[0])

        height = width // n_row
        groups = min(n_col, height // 16)
        thin = height // groups
        block = (rows, width)
        sem = pltpu.SemaphoreType.DMA
        scratch = {
            "panel": pltpu.VMEM((n_row,) + block, BF),
            "proj": pltpu.VMEM((n_row,) + block, BF),
            "pss": sem((2 * ro_n,)),
            "prs": sem((n_row,)),
            "weight": pltpu.VMEM((width, width), BF),
            "cot": pltpu.VMEM(block, BF),
            "ls": sem((3,)),
            "tile": pltpu.VMEM((2, rows, span), BF),
            "ts": sem((2,)),
            "ysend": pltpu.VMEM((co_n, ci_n - 1) + block, BF),
            "yrecv": pltpu.VMEM((co_n, ci_n - 1) + block, BF),
            "yss": sem((co_n, ci_n - 1, PIECES)),
            "yrs": sem((co_n, ci_n - 1, PIECES)),
            "mine": pltpu.VMEM((co_n,) + block, F32),
            "spread": pltpu.VMEM((n_col,) + block, BF),
            "lsend": pltpu.VMEM((co_n,) + block, BF),
            "rrecv": pltpu.VMEM((co_n,) + block, BF),
            "lrecv": pltpu.VMEM((co_n,) + block, BF),
            "lss": sem((co_n, PIECES)),
            "rrs": sem((co_n, PIECES)),
            "lrs": sem((co_n, PIECES)),
            "up": pltpu.VMEM((n_col,) + block, BF),
            "uss": sem((n_col, PIECES, ci_n + 1)),
            "urs": sem((n_col, PIECES)),
            "back": pltpu.VMEM((n_row,) + block, F32),
            "gw": pltpu.VMEM((width, width), F32),
            "gsend": pltpu.VMEM((n_row, height, width), BF),
            "grecv": pltpu.VMEM((n_row - 1, height, width), BF),
            "gss": sem((n_row - 1,)),
            "grs": sem((n_row - 1,)),
            "bsend": pltpu.VMEM((ro_n,) + block, BF),
            "brecv": pltpu.VMEM((ro_n,) + block, BF),
            "bss": sem((ro_n,)),
            "brs": sem((ro_n,)),
            "xsend": pltpu.VMEM((ro_n - 1,) + block, BF),
            "xrecv": pltpu.VMEM((ro_n - 1,) + block, BF),
            "xss": sem((ro_n - 1,)),
            "xrs": sem((ro_n - 1,)),
            "part": pltpu.VMEM((groups, thin, width), BF),
            "crecv": pltpu.VMEM((n_col, thin, width), BF),
            "css": sem((n_col - 1,)),
            "crs": sem((n_col,)),
            "full": pltpu.VMEM((n_row, height, width), BF),
            "dss": sem((groups,)),
            "drs": sem((groups,)),
            "ess": sem((n_row, groups)),
            "ers": sem((n_row, groups)),
        }
        names = list(scratch)

        def kernel(feat, w, a, cot, out, gfeat, gweight, *refs):
            layer(n_row, n_col, feat, w, a, cot, out, gfeat, gweight, dict(zip(names, refs)))

        def shapes(kind):
            return (
                jax.ShapeDtypeStruct(block, BF),
                jax.ShapeDtypeStruct(block, BF),
                jax.ShapeDtypeStruct((width, width), kind),
            )

        free = pl.BlockSpec(memory_space=pl.ANY)
        results = pl.pallas_call(
            kernel,
            out_shape=shapes(BF),
            in_specs=[free, free, free, free],
            out_specs=(vmem, vmem, vmem),
            scratch_shapes=[scratch[name] for name in names],
            compiler_params=pltpu.CompilerParams(
                collective_id=0, has_side_effects=True, vmem_limit_bytes=VMEM_LIMIT
            ),
        )(features, weight, dense, cotangent)
        return tuple(
            pl.pallas_call(
                finish, out_shape=shapes(F32), in_specs=[vmem] * 3, out_specs=(vmem, vmem, vmem)
            )(*results)
        )

    return jax.shard_map(
        shards,
        mesh=mesh,
        in_specs=(
            P(("col", "row"), None),
            P(),
            P("row", "col", None, None, None),
            P("row", "col", None),
            P("row", "col", None),
            P("row", "col"),
            P(("row", "col"), None),
        ),
        out_specs=(P(("row", "col"), None), P(("col", "row"), None), P()),
        check_vma=False,
    )
```

```python
import functools

import jax
import jax.numpy as jnp
from jax import lax
from jax.experimental import pallas as pl
from jax.experimental.pallas import tpu as pltpu
from jax.sharding import PartitionSpec as P

MESH = pl.DeviceIdType.MESH
BF = jnp.bfloat16
F32 = jnp.float32
VMEM_LIMIT = 60 * 1024 * 1024
PIECES = 2


def densify(values, rows, cols, count, dense):
    side = values.shape[1]
    per = dense.shape[1] // side

    def clear(j, carry):
        dense[j] = jnp.zeros(dense.shape[1:], dense.dtype)
        return carry

    lax.fori_loop(0, dense.shape[0], clear, 0)

    def add(k, carry):
        r, c = rows[k], cols[k]
        spot = (
            r // per,
            pl.ds(pl.multiple_of((r % per) * side, side), side),
            pl.ds(pl.multiple_of(c * side, side), side),
        )
        dense[spot] = (dense[spot].astype(F32) + values[k].astype(F32)).astype(dense.dtype)
        return carry

    lax.fori_loop(0, count[0], add, 0)


def dot(a, b, dims):
    return lax.dot_general(a, b, (dims, ((), ())), preferred_element_type=F32)


NN = ((1,), (0,))
TN = ((0,), (0,))
NT = ((1,), (1,))


def finish(out_in, gfeat_in, gweight_in, out, gfeat, gweight):
    out[...] = out_in[...]
    gfeat[...] = gfeat_in[...]
    gweight[...] = gweight_in[...].astype(F32)


def layer(n_row, n_col, feat, weight_in, dense, cot_in, out, gfeat, gweight, s):
    ri_n = 2
    ro_n = n_row // ri_n
    co_n = 4
    ci_n = n_col // co_n
    rows, width = feat.shape
    r, c = lax.axis_index("row"), lax.axis_index("col")
    ro, ri = r // ri_n, r % ri_n
    co, ci = c // ci_n, c % ci_n
    span = n_row * rows
    thick = rows // PIECES
    cuts = [pl.ds(h * thick, thick) for h in range(PIECES)]
    weight, cot = s["weight"], s["cot"]

    def send(src, dst, ss, rs, row, col):
        return pltpu.make_async_remote_copy(
            src_ref=src, dst_ref=dst, send_sem=ss, recv_sem=rs, device_id=(row, col), device_id_type=MESH
        )

    def arrived(dst, rs, ss):
        send(dst, dst, ss, rs, r, lax.rem(c + 1, n_col)).wait_recv()

    barrier = pltpu.get_barrier_semaphore()
    for d in range(1, n_row):
        pl.semaphore_signal(barrier, inc=1, device_id=(lax.rem(r + d, n_row), c), device_id_type=MESH)
    for d in range(1, n_col):
        pl.semaphore_signal(barrier, inc=1, device_id=(r, lax.rem(c + d, n_col)), device_id_type=MESH)
    loads = [
        pltpu.make_async_copy(feat, s["panel"].at[r], s["ls"].at[0]),
        pltpu.make_async_copy(weight_in, weight, s["ls"].at[1]),
        pltpu.make_async_copy(cot_in, cot, s["ls"].at[2]),
    ]
    for cp in loads:
        cp.start()
    pl.semaphore_wait(barrier, n_row + n_col - 2)

    mate = ro * ri_n + (1 - ri)
    pending = []
    for d in range(1, ro_n):
        peer = lax.rem(ro + d, ro_n) * ri_n + ri
        cp = send(feat, s["panel"].at[r], s["pss"].at[d - 1], s["prs"].at[r], peer, c)
        cp.start()
        pending.append(cp)
    cp = send(feat, s["panel"].at[r], s["pss"].at[ro_n - 1], s["prs"].at[r], mate, c)
    cp.start()
    pending.append(cp)

    def far(k):
        table = ((3, 2, 1, 0), (3, 0, 2, 1), (0, 3, 1, 2), (0, 1, 2, 3))

        def entry(pos):
            picked = jnp.int32(table[pos][co_n - 1])
            for q in range(co_n - 1):
                picked = jnp.where(k == q, table[pos][q], picked)
            return picked

        picked = entry(co_n - 1)
        for pos in range(co_n - 1):
            picked = jnp.where(co == pos, entry(pos), picked)
        return picked

    def fetch(j, slot):
        return pltpu.make_async_copy(dense.at[j], s["tile"].at[slot], s["ts"].at[slot])

    fetch(far(0) * ci_n + lax.rem(ci + 1, ci_n), 0).start()
    for cp in loads:
        cp.wait()

    def project(slot):
        s["proj"][slot] = dot(s["panel"][slot], weight[...], NN).astype(BF)

    project(r)
    for d in range(1, ro_n):
        slot = lax.rem(ro - d + ro_n, ro_n) * ri_n + ri
        arrived(s["panel"].at[slot], s["prs"].at[slot], s["pss"].at[0])
        cp = send(s["panel"].at[slot], s["panel"].at[slot], s["pss"].at[ro_n - 1 + d], s["prs"].at[slot], mate, c)
        cp.start()
        pending.append(cp)
        project(slot)
    for d in range(ro_n):
        slot = lax.rem(ro - d + ro_n, ro_n) * ri_n + (1 - ri)
        arrived(s["panel"].at[slot], s["prs"].at[slot], s["pss"].at[0])
        project(slot)

    def ycopy(t, d, h, col):
        return send(
            s["ysend"].at[t, d, cuts[h]], s["yrecv"].at[t, d, cuts[h]], s["yss"].at[t, d, h], s["yrs"].at[t, d, h],
            r, col,
        )

    def lcopy(t, h, name, col):
        return send(
            s["lsend"].at[t, cuts[h]], s[name + "recv"].at[t, cuts[h]], s["lss"].at[t, h], s[name + "rs"].at[t, h],
            r, col,
        )

    other = lax.rem(c + 1, n_col)

    def forward(k, carry):
        t = far(k)
        for d in list(range(1, ci_n)) + [0]:
            step = k * ci_n + (d - 1 if d else ci_n - 1)
            slot = step % 2
            target = lax.rem(ci + d, ci_n)
            j = t * ci_n + target
            ahead = step + 1
            if d:
                after = t * ci_n + lax.rem(ci + (d + 1) % ci_n, ci_n)
                fetch(after, ahead % 2).start()
            else:
                @pl.when(k < co_n - 1)
                def _():
                    fetch(far(k + 1) * ci_n + lax.rem(ci + 1, ci_n), ahead % 2).start()
            fetch(j, slot).wait()
            part = dot(s["tile"][slot], s["proj"][...].reshape(span, width), NN)
            if d:
                s["ysend"][t, d - 1] = part.astype(BF)
                for h in range(PIECES):
                    ycopy(t, d - 1, h, co * ci_n + target).start()
            else:
                s["mine"][t] = part
            s["spread"][j] = dot(s["tile"][slot], s["panel"][...].reshape(span, width), NN).astype(BF)
        return carry

    lax.fori_loop(0, co_n, forward, 0)

    def along(k, carry):
        t = far(k)
        for h in range(PIECES):
            cut = cuts[h]
            for d in range(1, ci_n):
                ycopy(t, d - 1, h, other).wait_recv()
                s["mine"][t, cut] = s["mine"][t, cut] + s["yrecv"][t, d - 1, cut].astype(F32)

            @pl.when(jnp.logical_and(t >= co, co > 0))
            def _():
                lcopy(t, h, "r", other).wait_recv()
                s["mine"][t, cut] = s["mine"][t, cut] + s["rrecv"][t, cut].astype(F32)

            @pl.when(jnp.logical_and(t <= co, co < co_n - 1))
            def _():
                lcopy(t, h, "l", other).wait_recv()
                s["mine"][t, cut] = s["mine"][t, cut] + s["lrecv"][t, cut].astype(F32)

            @pl.when(t != co)
            def _():
                s["lsend"][t, cut] = s["mine"][t, cut].astype(BF)

            @pl.when(t > co)
            def _():
                lcopy(t, h, "r", c + ci_n).start()

            @pl.when(t < co)
            def _():
                lcopy(t, h, "l", c - ci_n).start()

        return carry

    lax.fori_loop(0, co_n, along, 0)

    pre = s["mine"][co]
    sig = jax.nn.sigmoid(pre)
    s["up"][c] = (cot[...].astype(F32) * sig * (1.0 + pre * (1.0 - sig))).astype(BF)

    s["back"][...] = jnp.zeros(s["back"].shape, F32)
    s["gw"][...] = jnp.zeros(s["gw"].shape, F32)

    def upcopy(slot, h, kind, row, col):
        return send(
            s["up"].at[slot, cuts[h]], s["up"].at[slot, cuts[h]], s["uss"].at[slot, h, kind], s["urs"].at[slot, h],
            row, col,
        )

    def use_back(j, slot):
        fetch(j, slot).wait()
        u = s["up"][j]

        def piece(q, carry):
            cols = pl.ds(pl.multiple_of(q * rows, rows), rows)
            s["back"][q] = s["back"][q] + dot(s["tile"][slot, :, cols], u, TN)
            return carry

        lax.fori_loop(0, n_row, piece, 0)

    def use_gw(j):
        s["gw"][...] = s["gw"][...] + dot(s["spread"][j], s["up"][j], TN)

    def wait_up(j):
        for h in range(PIECES):
            upcopy(j, h, 0, r, other).wait_recv()

    def pass_on(k, h):
        t = far(co_n - 1 - k)
        j = t * ci_n + ci

        @pl.when(k > 0)
        def _():
            upcopy(j, h, 0, r, other).wait_recv()

        @pl.when(jnp.logical_and(t <= co, co < co_n - 1))
        def _():
            upcopy(j, h, 0, r, c + ci_n).start()

        @pl.when(jnp.logical_and(t >= co, co > 0))
        def _():
            upcopy(j, h, 1, r, c - ci_n).start()

        for d in range(1, ci_n):
            upcopy(j, h, 1 + d, r, co * ci_n + lax.rem(ci + d, ci_n)).start()

    def own_chunk(k):
        return far(co_n - 1 - k) * ci_n + ci

    def side_chunk(k, d):
        return far(co_n - 1 - k) * ci_n + lax.rem(ci + d, ci_n)

    def use_own(k):
        j = own_chunk(k)
        use_back(j, 0)
        use_gw(j)

    def use_sides(k):
        for d in range(1, ci_n):
            j = side_chunk(k, d)
            fetch(j, 1).start()
            wait_up(j)
            use_back(j, 1)
            use_gw(j)

    def backward(k, carry):
        @pl.when(k > 0)
        def _():
            fetch(own_chunk(k - 1), 0).start()

        for h in range(PIECES - 1):
            pass_on(k, h)

        @pl.when(k > 0)
        def _():
            use_own(k - 1)

        pass_on(k, PIECES - 1)

        @pl.when(k == 0)
        def _():
            value = s["mine"][co]
            out[...] = (value * jax.nn.sigmoid(value)).astype(BF)

        @pl.when(k > 1)
        def _():
            use_sides(k - 2)

        return carry

    lax.fori_loop(0, co_n, backward, 0)
    fetch(own_chunk(co_n - 1), 0).start()
    use_own(co_n - 1)
    use_sides(co_n - 2)
    for d in range(1, ci_n):
        last = side_chunk(co_n - 1, d)
        fetch(last, 1).start()
        if d < ci_n - 1:
            wait_up(last)
            use_back(last, 1)
            use_gw(last)

    def back_piece(h):
        u = s["up"][last, cuts[h]]

        def piece(q, carry):
            cols = pl.ds(pl.multiple_of(q * rows, rows), rows)
            s["back"][q] = s["back"][q] + dot(s["tile"][1, cuts[h], cols], u, TN)
            return carry

        lax.fori_loop(0, n_row, piece, 0)

    def gw_piece(h):
        s["gw"][...] = s["gw"][...] + dot(s["spread"][last, cuts[h]], s["up"][last, cuts[h]], TN)

    fetch(last, 1).wait()
    for h in range(PIECES):
        upcopy(last, h, 0, r, other).wait_recv()
        gw_piece(h)
        if h < PIECES - 1:
            back_piece(h)


    height = width // n_row
    s["gsend"][...] = s["gw"][...].astype(BF).reshape(n_row, height, width)
    for d in range(1, n_row):
        peer = lax.rem(r + d, n_row)
        cp = send(s["gsend"].at[peer], s["grecv"].at[d - 1], s["gss"].at[d - 1], s["grs"].at[d - 1], peer, c)
        cp.start()
        pending.append(cp)

    back_piece(PIECES - 1)

    for q in range(ro_n):
        d = lax.rem(ro + 1 + q, ro_n)
        s["bsend"][d] = s["back"][d * ri_n + (1 - ri)].astype(BF)
        cp = send(s["bsend"].at[d], s["brecv"].at[d], s["bss"].at[d], s["brs"].at[d], mate, c)
        cp.start()
        pending.append(cp)
    for q in range(1, ro_n):
        d = lax.rem(ro + q, ro_n)
        arrived(s["brecv"].at[d], s["brs"].at[d], s["bss"].at[d])
        s["xsend"][q - 1] = (s["back"][d * ri_n + ri] + s["brecv"][d].astype(F32)).astype(BF)
        cp = send(
            s["xsend"].at[q - 1], s["xrecv"].at[q - 1], s["xss"].at[q - 1], s["xrs"].at[q - 1], d * ri_n + ri, c
        )
        cp.start()
        pending.append(cp)
    arrived(s["brecv"].at[ro], s["brs"].at[ro], s["bss"].at[ro])

    groups = s["part"].shape[0]
    thin = s["part"].shape[1]
    total = s["gsend"][r].astype(F32)
    for d in range(1, n_row):
        arrived(s["grecv"].at[d - 1], s["grs"].at[d - 1], s["gss"].at[d - 1])
        total = total + s["grecv"][d - 1].astype(F32)
    s["part"][...] = total.astype(BF).reshape(groups, thin, width)
    own = c % groups
    for d in range(1, n_col):
        peer = lax.rem(c + d, n_col)
        cp = send(s["part"].at[peer % groups], s["crecv"].at[c], s["css"].at[d - 1], s["crs"].at[c], r, peer)
        cp.start()
        pending.append(cp)
    s["crecv"][c] = s["part"][own]

    grad = s["back"][r] + s["brecv"][ro].astype(F32)
    for q in range(1, ro_n):
        arrived(s["xrecv"].at[q - 1], s["xrs"].at[q - 1], s["xss"].at[q - 1])
        grad = grad + s["xrecv"][q - 1].astype(F32)
    gfeat[...] = dot(grad.astype(BF), weight[...], NT).astype(BF)

    for d in range(1, n_col):
        slot = lax.rem(c + d, n_col)
        arrived(s["crecv"].at[slot], s["crs"].at[slot], s["css"].at[0])
    total = s["crecv"][0].astype(F32)
    for q in range(1, n_col):
        total = total + s["crecv"][q].astype(F32)
    place = pl.ds(pl.multiple_of(own * thin, thin), thin)
    s["full"][r, place, :] = total.astype(BF)
    def strip(row, piece):
        return s["full"].at[row, pl.ds(pl.multiple_of(piece * thin, thin), thin), :]

    def spread_rows(piece):
        for d in range(1, n_row):
            peer = lax.rem(r + d, n_row)
            ref = strip(r, piece)
            cp = send(ref, ref, s["ess"].at[d, piece], s["ers"].at[r, piece], peer, c)
            cp.start()
            pending.append(cp)

    for d in range(1, groups):
        peer = (c // groups) * groups + lax.rem(own + d, groups)
        cp = send(strip(r, own), strip(r, own), s["dss"].at[d], s["drs"].at[own], r, peer)
        cp.start()
        pending.append(cp)
    spread_rows(own)
    for d in range(1, groups):
        slot = lax.rem(own + groups - d, groups)
        arrived(strip(r, slot), s["drs"].at[slot], s["dss"].at[0])
        spread_rows(slot)
    for d in range(1, n_row):
        row = lax.rem(r + d, n_row)
        for piece in range(groups):
            arrived(strip(row, piece), s["ers"].at[row, piece], s["ess"].at[0, 0])
    gweight[...] = s["full"][...].reshape(width, width)

    def left(k, carry):
        j = k * ci_n + ci
        for h in range(PIECES):
            for d in range(1, ci_n):
                ycopy(k, d - 1, h, other).wait_send()
                upcopy(j, h, 1 + d, r, other).wait_send()

            @pl.when(k != co)
            def _():
                lcopy(k, h, "r", other).wait_send()

            @pl.when(jnp.logical_and(k <= co, co < co_n - 1))
            def _():
                upcopy(j, h, 0, r, other).wait_send()

            @pl.when(jnp.logical_and(k >= co, co > 0))
            def _():
                upcopy(j, h, 1, r, other).wait_send()

        return carry

    lax.fori_loop(0, co_n, left, 0)
    for cp in pending:
        cp.wait_send()


def solution(mesh):
    n_row, n_col = mesh.shape["row"], mesh.shape["col"]

    def shards(features, weight, entry_values, block_rows, block_cols, entry_counts, cotangent):
        rows, width = features.shape
        span = n_row * rows
        co_n, ci_n, ro_n = 4, n_col // 4, n_row // 2
        smem = pl.BlockSpec(memory_space=pltpu.SMEM)
        vmem = pl.BlockSpec(memory_space=pltpu.VMEM)
        dense = pl.pallas_call(
            densify,
            out_shape=jax.ShapeDtypeStruct((n_col, rows, span), BF),
            in_specs=[vmem, smem, smem, smem],
            out_specs=vmem,
            compiler_params=pltpu.CompilerParams(vmem_limit_bytes=VMEM_LIMIT),
        )(entry_values[0, 0], block_rows[0, 0], block_cols[0, 0], entry_counts[0])

        height = width // n_row
        groups = min(n_col, height // 16)
        thin = height // groups
        block = (rows, width)
        sem = pltpu.SemaphoreType.DMA
        scratch = {
            "panel": pltpu.VMEM((n_row,) + block, BF),
            "proj": pltpu.VMEM((n_row,) + block, BF),
            "pss": sem((2 * ro_n,)),
            "prs": sem((n_row,)),
            "weight": pltpu.VMEM((width, width), BF),
            "cot": pltpu.VMEM(block, BF),
            "ls": sem((3,)),
            "tile": pltpu.VMEM((2, rows, span), BF),
            "ts": sem((2,)),
            "ysend": pltpu.VMEM((co_n, ci_n - 1) + block, BF),
            "yrecv": pltpu.VMEM((co_n, ci_n - 1) + block, BF),
            "yss": sem((co_n, ci_n - 1, PIECES)),
            "yrs": sem((co_n, ci_n - 1, PIECES)),
            "mine": pltpu.VMEM((co_n,) + block, F32),
            "spread": pltpu.VMEM((n_col,) + block, BF),
            "lsend": pltpu.VMEM((co_n,) + block, BF),
            "rrecv": pltpu.VMEM((co_n,) + block, BF),
            "lrecv": pltpu.VMEM((co_n,) + block, BF),
            "lss": sem((co_n, PIECES)),
            "rrs": sem((co_n, PIECES)),
            "lrs": sem((co_n, PIECES)),
            "up": pltpu.VMEM((n_col,) + block, BF),
            "uss": sem((n_col, PIECES, ci_n + 1)),
            "urs": sem((n_col, PIECES)),
            "back": pltpu.VMEM((n_row,) + block, F32),
            "gw": pltpu.VMEM((width, width), F32),
            "gsend": pltpu.VMEM((n_row, height, width), BF),
            "grecv": pltpu.VMEM((n_row - 1, height, width), BF),
            "gss": sem((n_row - 1,)),
            "grs": sem((n_row - 1,)),
            "bsend": pltpu.VMEM((ro_n,) + block, BF),
            "brecv": pltpu.VMEM((ro_n,) + block, BF),
            "bss": sem((ro_n,)),
            "brs": sem((ro_n,)),
            "xsend": pltpu.VMEM((ro_n - 1,) + block, BF),
            "xrecv": pltpu.VMEM((ro_n - 1,) + block, BF),
            "xss": sem((ro_n - 1,)),
            "xrs": sem((ro_n - 1,)),
            "part": pltpu.VMEM((groups, thin, width), BF),
            "crecv": pltpu.VMEM((n_col, thin, width), BF),
            "css": sem((n_col - 1,)),
            "crs": sem((n_col,)),
            "full": pltpu.VMEM((n_row, height, width), BF),
            "dss": sem((groups,)),
            "drs": sem((groups,)),
            "ess": sem((n_row, groups)),
            "ers": sem((n_row, groups)),
        }
        names = list(scratch)

        def kernel(feat, w, a, cot, out, gfeat, gweight, *refs):
            layer(n_row, n_col, feat, w, a, cot, out, gfeat, gweight, dict(zip(names, refs)))

        def shapes(kind):
            return (
                jax.ShapeDtypeStruct(block, BF),
                jax.ShapeDtypeStruct(block, BF),
                jax.ShapeDtypeStruct((width, width), kind),
            )

        free = pl.BlockSpec(memory_space=pl.ANY)
        results = pl.pallas_call(
            kernel,
            out_shape=shapes(BF),
            in_specs=[free, free, free, free],
            out_specs=(vmem, vmem, vmem),
            scratch_shapes=[scratch[name] for name in names],
            compiler_params=pltpu.CompilerParams(
                collective_id=0, has_side_effects=True, vmem_limit_bytes=VMEM_LIMIT
            ),
        )(features, weight, dense, cotangent)
        return tuple(
            pl.pallas_call(
                finish, out_shape=shapes(F32), in_specs=[vmem] * 3, out_specs=(vmem, vmem, vmem)
            )(*results)
        )

    return jax.shard_map(
        shards,
        mesh=mesh,
        in_specs=(
            P(("col", "row"), None),
            P(),
            P("row", "col", None, None, None),
            P("row", "col", None),
            P("row", "col", None),
            P("row", "col"),
            P(("row", "col"), None),
        ),
        out_specs=(P(("row", "col"), None), P(("col", "row"), None), P()),
        check_vma=False,
    )
```
